256 devices in a mesh: grp: 8 (over y, z_hi), dom: 32 (over z_lo, x, core).
Axes of the slice: x: 4, y: 4, z: 8 (z_hi: 2, z_lo: 4; z = z_hi * 4 + z_lo), core: 2. Of those that a mesh axis runs over, the one named last changes fastest.
Arguments:
- user_table: float32 [262144, 256], P(('grp', 'dom')), may hold values from -96 to 96
- user_accum: float32 [262144, 256], P(('grp', 'dom')), may hold values from 0.05 to 1
- item_table: float32 [262144, 256], P(('grp', 'dom')), may hold values from -11 to 11
- item_accum: float32 [262144, 256], P(('grp', 'dom')), may hold values from 0.05 to 1
- block_pick: int32 [2, 2, 256], P(None, None, ('grp', 'dom')), may hold values from 0 to 7
- positives: int32 [2, 2, 131072], P(None, None, ('grp', 'dom')), may hold values from 0 to 1023
- partners: int32 [2, 32], replicated, may hold values from 0 to 31, as said below
Outputs:
- users_out: float32 [262144, 256], P(('grp', 'dom'))
- user_accum_out: float32 [262144, 256], P(('grp', 'dom'))
- items_out: float32 [262144, 256], P(('grp', 'dom'))
- item_accum_out: float32 [262144, 256], P(('grp', 'dom'))
The draws below stay inside these ranges and needn't reach their ends.
Inputs may be any that keep to these rules, and one draw needn't show every extreme that they name: partners[b, d] equals d XOR 2**j_b for one whole number j_b of 0 to log2(32) - 1 in each bucket.
All inputs are finite; a program needn't handle non-finite values.
Results may differ from the reference program's by a relative error of at most 0.0008.
Values sent between devices are 32-bit elements; how exact they have to be, the bound alone decides.
No kernel may reach another device: no remote copies, remote signals or barrier semaphores. Data moves between devices by JAX's collectives and lax.ppermute only.
A program may use at most 64 MiB of HBM per device.

```python
import math
import jax
import jax.numpy as jnp
from jax import lax

D = 256
BLOCK = 128
BUCKETS = 2
INNER = 2
USR_DEV = 1024
ITEM_DEV = 1024
USER_SPAN = 512
USERS = 262144
ITEMS = 262144
BATCH = 1024
N_GRP = 8
N_DOM = 32
DEVICES = 256


def draw_user_table(key, part):
    sub_key = jax.random.fold_in(key, 1)
    return jnp.clip(0.5 * jax.random.normal(sub_key, (USERS, D), jnp.float32), -3.0, 3.0)


def draw_item_table(key, part):
    sub_key = jax.random.fold_in(key, 2)
    return jnp.clip(0.4 * jax.random.normal(sub_key, (ITEMS, D), jnp.float32), -2.4, 2.4)


def draw_partners(key, part):
    levels = N_DOM.bit_length() - 1
    level_pick = jax.random.randint(jax.random.fold_in(key, 3), (BUCKETS, 1), 0, levels, dtype=jnp.int32)
    masks = jnp.left_shift(jnp.ones_like(level_pick), level_pick)
    groups = jnp.arange(N_DOM, dtype=jnp.int32)[None, :]
    return jnp.bitwise_xor(groups, masks).astype(jnp.int32)


def set_ends(drawn, stream_key, least, largest):
    extent = drawn.shape
    index_at = [jax.random.randint(jax.random.fold_in(stream_key, axis), (), 0, extent[axis]) for axis in range(len(extent))]
    drawn = drawn.at[tuple(index_at)].set(least)
    longest = extent.index(max(extent))
    index_at[longest] = (index_at[longest] + 1) % extent[longest]
    return drawn.at[tuple(index_at)].set(largest)


def block_levels(stream_key, extent, cuts, least, largest):
    def one(dim, shards_of):
        heights = jax.random.uniform(jax.random.fold_in(jax.random.fold_in(stream_key, 6), dim), (shards_of,), jnp.float32, least / len(cuts), largest / len(cuts))
        return jnp.repeat(jnp.exp(heights), extent[dim] // shards_of).reshape((-1,) + (1,) * (len(extent) - dim - 1))

    level = one(*cuts[0])
    for cut in cuts[1:]:
        level = level * one(*cut)
    return level


def setup_inputs(seed: int = 0) -> dict:
    seeds = jax.random.split(jax.random.key(seed), 8)
    return {
        "user_table": draw_user_table(jax.random.fold_in(seeds[7], 71), 0),
        "user_accum": jnp.clip(jnp.exp(math.log(1.0) - 2.9957323 * jax.random.uniform(seeds[1], (USERS, D), jnp.float32) ** block_levels(seeds[1], (USERS, D), ((0, 256),), -0.2, 0.2)), 0.05, 1.0),
        "item_table": draw_item_table(jax.random.fold_in(seeds[7], 71), 0),
        "item_accum": jnp.clip(jnp.exp(math.log(1.0) - 2.9957323 * jax.random.uniform(seeds[3], (ITEMS, D), jnp.float32) ** block_levels(seeds[3], (ITEMS, D), ((0, 256),), -0.2, 0.2)), 0.05, 1.0),
        "block_pick": set_ends(jax.random.randint(seeds[4], (BUCKETS, INNER, DEVICES), 0, ITEM_DEV // BLOCK), jax.random.fold_in(seeds[4], 1), 0, (ITEM_DEV // BLOCK) - 1).astype(jnp.int32),
        "positives": set_ends(jax.random.randint(seeds[5], (BUCKETS, INNER, USER_SPAN * DEVICES), 0, BATCH), jax.random.fold_in(seeds[5], 1), 0, BATCH - 1).astype(jnp.int32),
        "partners": draw_partners(jax.random.fold_in(seeds[7], 71), 0),
    }


learn_rate = 0.3
epsilon = 1e-06

def adagrad(param, accum, grad):
    accum = accum + grad * grad
    return (param - learn_rate * grad / (jnp.sqrt(accum) + epsilon), accum)

def take_block(source, picked):
    return lax.dynamic_slice_in_dim(source, (picked * BLOCK).astype(jnp.int32), BLOCK, 0)

def put_block(source, update, picked):
    return lax.dynamic_update_slice_in_dim(source, update, (picked * BLOCK).astype(jnp.int32), 0)

def group_step(operands, sub_batch):
    users, uaccum, items, iaccum, picked, targets = operands
    user_span = USR_DEV // INNER
    first_user = sub_batch * user_span
    chosen = jax.vmap(take_block)(items, picked)
    chosen_acc = jax.vmap(take_block)(iaccum, picked)
    gathered = chosen.reshape(N_GRP * BLOCK, D)
    user_rows = users[:, first_user:first_user + user_span]
    user_acc = uaccum[:, first_user:first_user + user_span]
    scores = jnp.einsum('gud,bd->gub', user_rows, gathered, precision=lax.Precision.HIGHEST)
    softmax_rows = jax.nn.softmax(scores, axis=-1)
    onehot = (targets[:, :, None] == jnp.arange(N_GRP * BLOCK, dtype=jnp.int32)[None, None, :]).astype(jnp.float32)
    score_grad = softmax_rows - onehot
    grad_user = jnp.einsum('gub,bd->gud', score_grad, gathered, precision=lax.Precision.HIGHEST)
    grad_item = jnp.einsum('gub,gud->bd', score_grad, user_rows, precision=lax.Precision.HIGHEST).reshape(N_GRP, BLOCK, D)
    new_rows, new_acc = adagrad(user_rows, user_acc, grad_user)
    users = users.at[:, first_user:first_user + user_span].set(new_rows)
    uaccum = uaccum.at[:, first_user:first_user + user_span].set(new_acc)
    new_items, new_iacc = adagrad(chosen, chosen_acc, grad_item)
    items = jax.vmap(put_block)(items, new_items, picked)
    iaccum = jax.vmap(put_block)(iaccum, new_iacc, picked)
    return (users, uaccum, items, iaccum)

def regroup(source, per_device):
    return source.reshape(N_GRP, N_DOM, per_device, D).transpose(1, 0, 2, 3)

def restore(source):
    return source.transpose(1, 0, 2, 3).reshape(-1, D)

def reference(user_table, user_accum, item_table, item_accum, block_pick, positives, partners):
    user_span = USR_DEV // INNER
    users = regroup(user_table, USR_DEV)
    uaccum = regroup(user_accum, USR_DEV)
    items = regroup(item_table, ITEM_DEV)
    iaccum = regroup(item_accum, ITEM_DEV)
    for bucket in range(BUCKETS):
        for sub_batch in range(INNER):
            picked = block_pick[bucket, sub_batch].reshape(N_GRP, N_DOM).T
            targets = positives[bucket, sub_batch].reshape(N_GRP, N_DOM, user_span).transpose(1, 0, 2)
            users, uaccum, items, iaccum = lax.map(lambda operands: group_step(operands, sub_batch), (users, uaccum, items, iaccum, picked, targets))
        partner_row = partners[bucket].astype(jnp.int32)
        items = items[partner_row]
        iaccum = iaccum[partner_row]
    return (restore(users), restore(uaccum), restore(items), restore(iaccum))
```

```python
import functools

import jax
import jax.numpy as jnp
from jax import lax
from jax.experimental import pallas as pl
from jax.experimental.pallas import tpu as pltpu
from jax.sharding import PartitionSpec as P

BLOCK = 128
BUCKETS = 2
INNER = 2
RING = 4

learn_rate = 0.3
epsilon = 1e-06

NT = (((1,), (1,)), ((), ()))
NN = (((1,), (0,)), ((), ()))
TN = (((0,), (0,)), ((), ()))
VMEM_BYTES = 48 * 2**20
CHUNK = 4 * BLOCK


def halves(x):
    high = x.astype(jnp.bfloat16)
    return high, (x - high.astype(jnp.float32)).astype(jnp.bfloat16)


def product(a, b, dims):
    def dot(p, q):
        return lax.dot_general(p, q, dims, preferred_element_type=jnp.float32)

    return dot(a[0], b[0]) + (dot(a[0], b[1]) + dot(a[1], b[0]))


def fold(x, op):
    return op(x.reshape(x.shape[0] // 8, 8, x.shape[1]), axis=0)


def split_blocks(blocks, high, low):
    for i, ref in enumerate(blocks):
        rows = slice(i * BLOCK, (i + 1) * BLOCK)
        high[rows, :], low[rows, :] = halves(ref[...])


def grad_kernel(ids, targets, users, *refs):
    count = (len(refs) - 6) // 2
    blocks, sums = refs[:count], refs[count : 2 * count]
    grad_high, grad_low, high, low, scores, totals = refs[2 * count :]
    split_blocks(blocks, high, low)
    user_parts = halves(users[...])
    span = users.shape[0]
    per_step = CHUNK // BLOCK
    steps = count // per_step

    def rows_of(step):
        return pl.ds(pl.multiple_of(step * CHUNK, CHUNK), CHUNK)

    def score(step, top):
        rows = rows_of(step)
        part = product((high[rows, :], low[rows, :]), user_parts, NT)
        scores[rows, :] = part
        return jnp.maximum(top, fold(part, jnp.max))

    top = lax.fori_loop(0, steps, score, jnp.full((8, span), -jnp.inf, jnp.float32))
    top = jnp.max(top, axis=0, keepdims=True)

    def power(step, total):
        rows = rows_of(step)
        part = jnp.exp(scores[rows, :] - top)
        scores[rows, :] = part
        return total + fold(part, jnp.sum)

    total = lax.fori_loop(0, steps, power, jnp.zeros((8, span), jnp.float32))
    scale = 1.0 / jnp.sum(total, axis=0, keepdims=True)
    target = targets[...]
    row = lax.broadcasted_iota(jnp.int32, (BLOCK, span), 0)

    def grads(step, carry):
        rows = rows_of(step)
        hits = [row + ids[step * per_step + k] * BLOCK == target for k in range(per_step)]
        hit = jnp.concatenate([jnp.where(h, 1.0, 0.0) for h in hits], axis=0)
        parts = halves(scores[rows, :] * scale - hit)
        grad_high[rows, :] = parts[0]
        grad_low[rows, :] = parts[1]
        totals[rows, :] = product(parts, user_parts, NN)
        return carry

    lax.fori_loop(0, steps, grads, 0)
    for i in range(count):
        sums[i][...] = totals[i * BLOCK : (i + 1) * BLOCK, :]


def user_kernel(grad_high, grad_low, users, accum, *refs):
    count = len(refs) - 4
    blocks, (new_users, new_accum, high, low) = refs[:count], refs[count:]
    split_blocks(blocks, high, low)
    grad = product((grad_high[...], grad_low[...]), (high[...], low[...]), TN)
    updated, total = adagrad(users[...], accum[...], grad)
    new_users[...] = updated
    new_accum[...] = total


def whole(shape):
    return pl.BlockSpec(shape, lambda i: (0, 0))


def item_grads(ids, targets, users, half, blocks):
    count, (span, width) = len(blocks), (targets.shape[1], blocks[0].shape[1])
    each = whole((BLOCK, width))
    coded = whole((count * BLOCK, span))
    out = pl.pallas_call(
        grad_kernel,
        grid=(1,),
        out_shape=[jax.ShapeDtypeStruct((BLOCK, width), jnp.float32)] * count
        + [jax.ShapeDtypeStruct((count * BLOCK, span), jnp.bfloat16)] * 2,
        in_specs=[
            pl.BlockSpec(memory_space=pltpu.SMEM),
            whole((1, span)),
            pl.BlockSpec((span, width), lambda i: (half, 0)),
        ]
        + [each] * count,
        out_specs=[each] * count + [coded] * 2,
        scratch_shapes=[pltpu.VMEM((count * BLOCK, width), jnp.bfloat16)] * 2
        + [
            pltpu.VMEM((count * BLOCK, span), jnp.float32),
            pltpu.VMEM((count * BLOCK, width), jnp.float32),
        ],
        compiler_params=pltpu.CompilerParams(vmem_limit_bytes=VMEM_BYTES),
        cost_estimate=pl.CostEstimate(
            flops=12 * span * count * BLOCK * width,
            bytes_accessed=5 * 2**20,
            transcendentals=span * count * BLOCK,
        ),
    )(ids, targets, users, *blocks)
    return out[:count], out[count], out[count + 1]


def user_update(grad_high, grad_low, users, accum, half, blocks):
    count, (span, width) = len(blocks), (grad_high.shape[1], blocks[0].shape[1])
    coded = whole(grad_high.shape)
    part = pl.BlockSpec((span, width), lambda i: (half, 0))
    shape = jax.ShapeDtypeStruct((span, width), jnp.float32)
    return pl.pallas_call(
        user_kernel,
        grid=(1,),
        out_shape=[shape] * 2,
        in_specs=[coded, coded, part, part] + [whole((BLOCK, width))] * count,
        out_specs=[whole((span, width))] * 2,
        scratch_shapes=[pltpu.VMEM((count * BLOCK, width), jnp.bfloat16)] * 2,
        compiler_params=pltpu.CompilerParams(vmem_limit_bytes=VMEM_BYTES),
        cost_estimate=pl.CostEstimate(
            flops=6 * span * count * BLOCK * width,
            bytes_accessed=5 * 2**20,
            transcendentals=span * width,
        ),
    )(grad_high, grad_low, users, accum, *blocks)


def shifted(value, step, flip):
    route = []
    for place in range(RING):
        for side in range(2):
            route.append((2 * place + side, 2 * ((place + step) % RING) + (side ^ flip)))
    return lax.ppermute(value, "grp", route)


def traded(value, mask):
    count = lax.axis_size("dom")
    return lax.ppermute(value, "dom", [(d, d ^ mask) for d in range(count)])


def traded_by(mask, masks, values):
    def along(values, mask):
        return tuple(traded(value, mask) for value in values) if mask else values

    index = sum(jnp.where(mask == m, i, 0) for i, m in enumerate(masks))
    return lax.switch(index, [functools.partial(along, mask=m) for m in masks], values)


def adagrad(param, accum, grad):
    accum = accum + grad * grad
    return (param - learn_rate * grad / (jnp.sqrt(accum) + epsilon), accum)


STEPS = (1, 3, 2)


def gathered(block):
    other = shifted(block, 0, 1)
    near = [shifted(block, -step, 0) for step in STEPS]
    far = [shifted(other, -step, 0) for step in STEPS]
    return [block] + near + [other] + far


def reduced(sums):
    far = [shifted(sums[5 + k], step, 0) for k, step in enumerate(STEPS)]
    crossed = shifted(sums[4] + far[0] + far[1] + far[2], 0, 1)
    near = [shifted(sums[1 + k], step, 0) for k, step in enumerate(STEPS)]
    return (sums[0] + near[0] + near[1] + near[2]) + crossed


def take(table, pick):
    return lax.dynamic_slice_in_dim(table, pick * BLOCK, BLOCK, 0)


def put(table, rows, pick):
    return lax.dynamic_update_slice_in_dim(table, rows, pick * BLOCK, 0)


def newest(pick, old, done):
    for earlier, new in done:
        old = tuple(jnp.where(earlier == pick, n, o) for n, o in zip(new, old))
    return old


def train(ids, chosen, users, half, targets):
    blocks = gathered(chosen[0])
    sums, high, low = item_grads(ids, targets, users[0], half, blocks)
    new_users = user_update(high, low, users[0], users[1], half, blocks)
    return new_users, adagrad(chosen[0], chosen[1], reduced(sums))


def body(user_table, user_accum, item_table, item_accum, block_pick, positives, partners):
    position = lax.axis_index("dom")
    levels = lax.axis_size("dom").bit_length() - 1
    singles = [1 << i for i in range(levels)]
    pairs = [0] + [1 << i | 1 << j for i in range(levels) for j in range(i)]
    span = user_table.shape[0] // INNER
    index = lax.axis_index("grp")
    place, side = index // 2, index % 2
    ids = jnp.stack(
        [(place + step) % RING * 2 + (side ^ flip) for flip in range(2) for step in (0,) + STEPS]
    ).astype(jnp.int32)
    targets = [
        [positives[bucket, sub].reshape(1, span) for sub in range(INNER)]
        for bucket in range(BUCKETS)
    ]
    mask = [jnp.bitwise_xor(partners[bucket, position], position) for bucket in range(BUCKETS)]
    picks = block_pick[:, :, 0]
    all_picks = lax.all_gather(picks[1], "dom")
    tables = (item_table, item_accum)

    done, users = [], []
    for sub in range(INNER):
        pick = picks[0, sub]
        chosen = newest(pick, tuple(take(t, pick) for t in tables), done)
        new_users, new = train(ids, chosen, (user_table, user_accum), sub, targets[0][sub])
        users.append(new_users)
        done.append((pick, new))

    sent = []
    for sub in range(INNER):
        wanted = all_picks[jnp.bitwise_xor(position, mask[0]), sub]
        sent += newest(wanted, tuple(take(t, wanted) for t in tables), done)
    (got,) = traded_by(mask[0], singles, (jnp.concatenate(sent),))
    got = [got[i * BLOCK : (i + 1) * BLOCK] for i in range(2 * INNER)]
    for pick, new in done:
        tables = tuple(put(t, n, pick) for t, n in zip(tables, new))
    tables = traded_by(jnp.bitwise_xor(mask[0], mask[1]), pairs, tables)

    done, last = [], []
    for sub in range(INNER):
        pick = picks[1, sub]
        chosen = newest(pick, tuple(got[2 * sub : 2 * sub + 2]), done)
        new_users, new = train(ids, chosen, users[sub], 0, targets[1][sub])
        last.append(new_users)
        done.append((pick, new))

    (got,) = traded_by(mask[1], singles, (jnp.concatenate([n for _, new in done for n in new]),))
    for sub in range(INNER):
        pick = all_picks[jnp.bitwise_xor(position, mask[1]), sub]
        new = [got[(2 * sub + k) * BLOCK : (2 * sub + k + 1) * BLOCK] for k in range(2)]
        tables = tuple(put(t, n, pick) for t, n in zip(tables, new))
    return tuple(jnp.concatenate([a, b]) for a, b in zip(*last)) + tables


def solution(mesh):
    placed = (
        P(("grp", "dom"), None),
        P(("grp", "dom"), None),
        P(("grp", "dom"), None),
        P(("grp", "dom"), None),
        P(None, None, ("grp", "dom")),
        P(None, None, ("grp", "dom")),
        P(),
    )
    return jax.shard_map(
        body,
        mesh=mesh,
        in_specs=placed,
        out_specs=(P(("grp", "dom"), None),) * 4,
        check_vma=False,
    )
```

```python
import functools

import jax
import jax.numpy as jnp
from jax import lax
from jax.experimental import pallas as pl
from jax.experimental.pallas import tpu as pltpu
from jax.sharding import PartitionSpec as P

BLOCK = 128
BLOCKS = 8
LEVELS = 5
BUCKETS = 2
INNER = 2
RING = 4

learn_rate = 0.3
epsilon = 1e-06

NT = (((1,), (1,)), ((), ()))
NN = (((1,), (0,)), ((), ()))
TN = (((0,), (0,)), ((), ()))
VMEM_BYTES = 24 * 2**20
STEPS = (1, 3, 2)


def halves(x):
    high = x.astype(jnp.bfloat16)
    return high, (x - high.astype(jnp.float32)).astype(jnp.bfloat16)


def product(a, b, dims):
    def dot(p, q):
        return lax.dot_general(p, q, dims, preferred_element_type=jnp.float32)

    return dot(a[0], b[0]) + (dot(a[0], b[1]) + dot(a[1], b[0]))


def fold(x, op):
    return op(x.reshape(x.shape[0] // 8, 8, x.shape[1]), axis=0)


def train_kernel(targets, users, accum, *refs):
    blocks, refs = refs[:BLOCKS], refs[-BLOCKS - 7 :]
    sums, (new_users, new_accum, high, low, scores, grad_high, grad_low) = refs[:BLOCKS], refs[BLOCKS:]
    for i, ref in enumerate(blocks):
        rows = slice(i * BLOCK, (i + 1) * BLOCK)
        high[rows, :], low[rows, :] = halves(ref[...])
    user_parts = halves(users[...])
    span = users.shape[0]
    chunk = RING * BLOCK

    def rows_of(flip):
        return pl.ds(pl.multiple_of(flip * chunk, chunk), chunk)

    def score(flip, top):
        rows = rows_of(flip)
        part = product((high[rows, :], low[rows, :]), user_parts, NT)
        scores[rows, :] = part
        return jnp.maximum(top, fold(part, jnp.max))

    top = lax.fori_loop(0, 2, score, jnp.full((8, span), -jnp.inf, jnp.float32))
    top = jnp.max(top, axis=0, keepdims=True)

    def power(flip, total):
        rows = rows_of(flip)
        part = jnp.exp(scores[rows, :] - top)
        scores[rows, :] = part
        return total + fold(part, jnp.sum)

    total = lax.fori_loop(0, 2, power, jnp.zeros((8, span), jnp.float32))
    scale = 1.0 / jnp.sum(total, axis=0, keepdims=True)
    index = lax.axis_index("grp")
    place, side = index // 2, index % 2
    target = targets[...]
    row = lax.broadcasted_iota(jnp.int32, (BLOCK, span), 0)

    def grads(flip, carry):
        rows = rows_of(flip)
        hits = []
        for step in (0,) + STEPS:
            block = (place + step) % RING * 2 + (side + flip) % 2
            hits.append(jnp.where(row + block * BLOCK == target, 1.0, 0.0))
        parts = halves(scores[rows, :] * scale - jnp.concatenate(hits, axis=0))
        grad_high[rows, :], grad_low[rows, :] = parts
        scores[rows, : users.shape[1]] = product(parts, user_parts, NN)
        return carry

    lax.fori_loop(0, 2, grads, 0)
    for i in range(BLOCKS):
        sums[i][...] = scores[i * BLOCK : (i + 1) * BLOCK, : users.shape[1]]
    grad = product((grad_high[...], grad_low[...]), (high[...], low[...]), TN)
    new_users[...], new_accum[...] = adagrad(users[...], accum[...], grad)


def whole(shape):
    return pl.BlockSpec(shape, lambda i: (0, 0))


def train_call(targets, tables, half, blocks, into, full):
    (block, width), span = blocks[0].shape, targets.shape[1]
    part = pl.BlockSpec((span, width), lambda i: (half, 0))
    result = jax.ShapeDtypeStruct((span * (INNER if full else 1), width), jnp.float32)
    place = pl.BlockSpec((span, width), lambda i: (half if full else 0, 0))
    source = part if tables[0].shape[0] > span else whole((span, width))
    rows = BLOCKS * block
    out = pl.pallas_call(
        train_kernel,
        grid=(1,),
        out_shape=[jax.ShapeDtypeStruct((block, width), jnp.float32)] * BLOCKS + [result] * 2,
        in_specs=[whole((1, span)), source, source]
        + [whole((block, width))] * BLOCKS
        + [pl.BlockSpec(memory_space=pl.ANY)] * len(into),
        out_specs=[whole((block, width))] * BLOCKS + [place] * 2,
        scratch_shapes=[pltpu.VMEM((rows, width), jnp.bfloat16)] * 2
        + [pltpu.VMEM((rows, span), jnp.float32)]
        + [pltpu.VMEM((rows, span), jnp.bfloat16)] * 2,
        input_output_aliases={3 + BLOCKS + k: BLOCKS + k for k in range(len(into))},
        compiler_params=pltpu.CompilerParams(vmem_limit_bytes=VMEM_BYTES),
        cost_estimate=pl.CostEstimate(
            flops=18 * span * rows * width,
            bytes_accessed=6 * 2**20,
            transcendentals=span * rows,
        ),
    )(targets, *tables, *blocks, *into)
    return out[:BLOCKS], tuple(out[BLOCKS:])


def slots(picks):
    first = picks[0]
    second = jnp.where(picks[1] == first, jnp.where(first == 0, 1, 0), picks[1])
    low, high = jnp.minimum(first, second), jnp.maximum(first, second)
    others = []
    for k in range(BLOCKS - 2):
        at = k + (k >= low).astype(jnp.int32)
        others.append(at + (at >= high).astype(jnp.int32))
    return first, second, others


def at_block(block):
    return pl.ds(pl.multiple_of(block * BLOCK, BLOCK), BLOCK)


def pack_kernel(changed, wanted, items, accum, *refs):
    done, sent, chunks = refs[:4], refs[4], refs[5:]
    first, second, others = slots((wanted[0], wanted[1]))
    count = len(others) // 2

    def copy(block, kind, ref, at):
        rows = slice(at * BLOCK, (at + 1) * BLOCK)
        ref[rows, :] = (items, accum)[kind][at_block(block), :]
        for sub in range(INNER):

            @pl.when(block == changed[sub])
            def _():
                ref[rows, :] = done[2 * sub + kind][...]

    for kind in range(2):
        copy(first, kind, sent, kind)
        copy(second, kind, sent, 2 + kind)
        for k, block in enumerate(others):
            copy(block, kind, chunks[2 * kind + k // count], k % count)
    for k, block in enumerate((first, second)):
        at = count * BLOCK + 8 * k
        chunks[0][at : at + 8, :] = jnp.full((8, items.shape[1]), block.astype(jnp.float32))


def pack(changed, wanted, items, accum, done):
    width = items.shape[1]
    heights = [4 * BLOCK, 3 * BLOCK + 16] + [3 * BLOCK] * 3
    shapes = [(h, width) for h in heights]
    smem = pl.BlockSpec(memory_space=pltpu.SMEM)
    return pl.pallas_call(
        pack_kernel,
        grid=(1,),
        out_shape=[jax.ShapeDtypeStruct(shape, jnp.float32) for shape in shapes],
        in_specs=[smem, smem] + [whole(items.shape)] * 2 + [whole((BLOCK, width))] * 4,
        out_specs=[whole(shape) for shape in shapes],
        compiler_params=pltpu.CompilerParams(vmem_limit_bytes=VMEM_BYTES),
        cost_estimate=pl.CostEstimate(flops=0, bytes_accessed=4 * 2**20, transcendentals=0),
    )(changed, wanted, items, accum, *done)


def place_kernel(pair, got, *refs):
    chunks, tables = refs[:4], refs[4:]
    first, second, others = slots((pair[0], pair[1]))
    count = len(others) // 2
    for kind in range(2):
        for k, block in enumerate(others):
            rows = slice(k % count * BLOCK, (k % count + 1) * BLOCK)
            tables[kind][at_block(block), :] = chunks[2 * kind + k // count][rows, :]
        for k, block in enumerate((first, second)):
            at = (2 * k + kind) * BLOCK
            tables[kind][at_block(block), :] = got[at : at + BLOCK, :]


def place_all(pair, got, chunks):
    shape = (BLOCKS * BLOCK, got.shape[1])
    return pl.pallas_call(
        place_kernel,
        grid=(1,),
        out_shape=[jax.ShapeDtypeStruct(shape, jnp.float32)] * 2,
        in_specs=[pl.BlockSpec(memory_space=pltpu.SMEM), whole(got.shape)]
        + [whole(chunk.shape) for chunk in chunks],
        out_specs=[whole(shape)] * 2,
        compiler_params=pltpu.CompilerParams(vmem_limit_bytes=VMEM_BYTES),
        cost_estimate=pl.CostEstimate(flops=0, bytes_accessed=4 * 2**20, transcendentals=0),
    )(pair, got, *chunks)


def plan_kernel(partners, out):
    position = lax.axis_index("dom")
    level = []
    for bucket in range(BUCKETS):
        mask = partners[bucket, position] ^ position
        level.append(sum((mask >> bit & 1) * bit for bit in range(1, LEVELS)))
    low, high = jnp.minimum(*level), jnp.maximum(*level)
    out[0], out[1] = level
    out[2] = jnp.where(low == high, 0, 1 + high * (high - 1) // 2 + low)


def plan(partners):
    smem = pl.BlockSpec(memory_space=pltpu.SMEM)
    return pl.pallas_call(
        plan_kernel,
        out_shape=jax.ShapeDtypeStruct((3,), jnp.int32),
        in_specs=[smem],
        out_specs=smem,
    )(partners)


def shifted(value, step, flip):
    route = []
    for place in range(RING):
        for side in range(2):
            route.append((2 * place + side, 2 * ((place + step) % RING) + (side ^ flip)))
    return lax.ppermute(value, "grp", route)


def traded(value, mask):
    count = lax.axis_size("dom")
    return lax.ppermute(value, "dom", [(d, d ^ mask) for d in range(count)])


def by_index(index, masks, act, *values):
    return lax.switch(index, [functools.partial(act, mask=m) for m in masks], *values)


def adagrad(param, accum, grad):
    accum = accum + grad * grad
    return (param - learn_rate * grad / (jnp.sqrt(accum) + epsilon), accum)


def crossed(value):
    return shifted(value, 0, 1)


def gathered(block, cross):
    near = [shifted(block, -step, 0) for step in STEPS]
    other = cross(block)
    far = [shifted(other, -step, 0) for step in STEPS]
    return [block] + near + [other] + far


def reduced(sums, cross):
    far = [shifted(sums[5 + k], step, 0) for k, step in enumerate(STEPS)]
    near = [shifted(sums[1 + k], step, 0) for k, step in enumerate(STEPS)]
    other = cross(sums[4] + far[0] + far[1] + far[2])
    return (sums[0] + near[0] + near[1] + near[2]) + other


def take(table, pick):
    return lax.dynamic_slice_in_dim(table, pick * BLOCK, BLOCK, 0)


def newest(again, new, old):
    return tuple(jnp.where(again, n, o) for n, o in zip(new, old))


def train(chosen, tables, half, targets, cross, into=(), full=False):
    blocks = gathered(chosen[0], cross)
    sums, users = train_call(targets, tables, half, blocks, into, full)
    return users, adagrad(chosen[0], chosen[1], reduced(sums, cross))


def body(user_table, user_accum, item_table, item_accum, block_pick, positives, partners):
    singles = [1 << i for i in range(LEVELS)]
    pairs = [0] + [1 << i | 1 << j for i in range(LEVELS) for j in range(i)]
    span = user_table.shape[0] // INNER
    targets = [
        [positives[bucket, sub].reshape(1, span) for sub in range(INNER)]
        for bucket in range(BUCKETS)
    ]
    picks = block_pick[:, :, 0]
    again = picks[:, 0] == picks[:, 1]
    tables = (item_table, item_accum)

    chosen = tuple(take(t, picks[0, 0]) for t in tables)
    users0, new0 = train(chosen, (user_table, user_accum), 0, targets[0][0], crossed)
    level = plan(partners)
    wanted = by_index(level[0], singles, traded, picks[1])
    chosen = newest(again[0], new0, tuple(take(t, picks[0, 1]) for t in tables))
    users1, new1 = train(chosen, (user_table, user_accum), 1, targets[0][1], crossed)

    sent, *chunks = pack(picks[0], wanted, *tables, new0 + new1)
    got = by_index(level[0], singles, traded, sent)
    got = tuple(got[i * BLOCK : (i + 1) * BLOCK] for i in range(4))
    arrived = []

    def cross_and_send(value):
        def act(value, chunk, mask):
            return crossed(value), traded(chunk, mask) if mask else chunk

        other, chunk = by_index(level[2], pairs, act, value, chunks[len(arrived)])
        arrived.append(chunk)
        return other

    users, new0 = train(got[:2], users0, 0, targets[1][0], cross_and_send, full=True)
    chosen = newest(again[1], new0, got[2:])
    users, new1 = train(
        chosen, users1, 1, targets[1][1], cross_and_send, into=users, full=True
    )

    last = newest(again[1], new1, new0) + newest(again[1], got[2:], new1)
    got = by_index(level[1], singles, traded, jnp.concatenate(last))
    at = arrived[0].shape[0] - 16
    pair = arrived[0][at::8, 0].astype(jnp.int32)
    return users + tuple(place_all(pair, got, arrived))


def solution(mesh):
    placed = (
        P(("grp", "dom"), None),
        P(("grp", "dom"), None),
        P(("grp", "dom"), None),
        P(("grp", "dom"), None),
        P(None, None, ("grp", "dom")),
        P(None, None, ("grp", "dom")),
        P(),
    )
    return jax.shard_map(
        body,
        mesh=mesh,
        in_specs=placed,
        out_specs=(P(("grp", "dom"), None),) * 4,
        check_vma=False,
    )
```

```python
import functools

import jax
import jax.numpy as jnp
from jax import lax
from jax.experimental import pallas as pl
from jax.experimental.pallas import tpu as pltpu
from jax.sharding import PartitionSpec as P

BLOCK = 128
BLOCKS = 8
LEVELS = 5
BUCKETS = 2
INNER = 2
RING = 4

learn_rate = 0.3
epsilon = 1e-06

NT = (((1,), (1,)), ((), ()))
NN = (((1,), (0,)), ((), ()))
TN = (((0,), (0,)), ((), ()))
VMEM_BYTES = 24 * 2**20
STEPS = (1, 3, 2)


def halves(x):
    high = x.astype(jnp.bfloat16)
    return high, (x - high.astype(jnp.float32)).astype(jnp.bfloat16)


def product(a, b, dims):
    def dot(p, q):
        return lax.dot_general(p, q, dims, preferred_element_type=jnp.float32)

    return dot(a[0], b[0]) + (dot(a[0], b[1]) + dot(a[1], b[0]))


def fold(x, op):
    return op(x.reshape(x.shape[0] // 8, 8, x.shape[1]), axis=0)


def train_kernel(targets, users, accum, *refs):
    blocks, refs = refs[:BLOCKS], refs[-BLOCKS - 7 :]
    sums, (new_users, new_accum, high, low, scores, grad_high, grad_low) = refs[:BLOCKS], refs[BLOCKS:]
    for i, ref in enumerate(blocks):
        rows = slice(i * BLOCK, (i + 1) * BLOCK)
        high[rows, :], low[rows, :] = halves(ref[...])
    user_parts = halves(users[...])
    span = users.shape[0]
    chunk = RING * BLOCK

    def rows_of(flip):
        return pl.ds(pl.multiple_of(flip * chunk, chunk), chunk)

    def score(flip, top):
        rows = rows_of(flip)
        part = product((high[rows, :], low[rows, :]), user_parts, NT)
        scores[rows, :] = part
        return jnp.maximum(top, fold(part, jnp.max))

    top = lax.fori_loop(0, 2, score, jnp.full((8, span), -jnp.inf, jnp.float32))
    top = jnp.max(top, axis=0, keepdims=True)

    def power(flip, total):
        rows = rows_of(flip)
        part = jnp.exp(scores[rows, :] - top)
        scores[rows, :] = part
        return total + fold(part, jnp.sum)

    total = lax.fori_loop(0, 2, power, jnp.zeros((8, span), jnp.float32))
    scale = 1.0 / jnp.sum(total, axis=0, keepdims=True)
    index = lax.axis_index("grp")
    place, side = index // 2, index % 2
    target = targets[...]
    row = lax.broadcasted_iota(jnp.int32, (BLOCK, span), 0)

    def grads(flip, carry):
        rows = rows_of(flip)
        hits = []
        for step in (0,) + STEPS:
            block = (place + step) % RING * 2 + (side + flip) % 2
            hits.append(jnp.where(row + block * BLOCK == target, 1.0, 0.0))
        parts = halves(scores[rows, :] * scale - jnp.concatenate(hits, axis=0))
        grad_high[rows, :], grad_low[rows, :] = parts
        scores[rows, : users.shape[1]] = product(parts, user_parts, NN)
        return carry

    lax.fori_loop(0, 2, grads, 0)
    for i in range(BLOCKS):
        sums[i][...] = scores[i * BLOCK : (i + 1) * BLOCK, : users.shape[1]]
    grad = product((grad_high[...], grad_low[...]), (high[...], low[...]), TN)
    new_users[...], new_accum[...] = adagrad(users[...], accum[...], grad)


def whole(shape):
    return pl.BlockSpec(shape, lambda i: (0, 0))


def train_call(targets, tables, half, blocks, into, full):
    (block, width), span = blocks[0].shape, targets.shape[1]
    part = pl.BlockSpec((span, width), lambda i: (half, 0))
    result = jax.ShapeDtypeStruct((span * (INNER if full else 1), width), jnp.float32)
    place = pl.BlockSpec((span, width), lambda i: (half if full else 0, 0))
    source = part if tables[0].shape[0] > span else whole((span, width))
    rows = BLOCKS * block
    out = pl.pallas_call(
        train_kernel,
        grid=(1,),
        out_shape=[jax.ShapeDtypeStruct((block, width), jnp.float32)] * BLOCKS + [result] * 2,
        in_specs=[whole((1, span)), source, source]
        + [whole((block, width))] * BLOCKS
        + [pl.BlockSpec(memory_space=pl.ANY)] * len(into),
        out_specs=[whole((block, width))] * BLOCKS + [place] * 2,
        scratch_shapes=[pltpu.VMEM((rows, width), jnp.bfloat16)] * 2
        + [pltpu.VMEM((rows, span), jnp.float32)]
        + [pltpu.VMEM((rows, span), jnp.bfloat16)] * 2,
        input_output_aliases={3 + BLOCKS + k: BLOCKS + k for k in range(len(into))},
        compiler_params=pltpu.CompilerParams(vmem_limit_bytes=VMEM_BYTES),
        cost_estimate=pl.CostEstimate(
            flops=18 * span * rows * width,
            bytes_accessed=6 * 2**20,
            transcendentals=span * rows,
        ),
    )(targets, *tables, *blocks, *into)
    return out[:BLOCKS], tuple(out[BLOCKS:])


def slots(picks):
    first = picks[0]
    second = jnp.where(picks[1] == first, jnp.where(first == 0, 1, 0), picks[1])
    low, high = jnp.minimum(first, second), jnp.maximum(first, second)
    others = []
    for k in range(BLOCKS - 2):
        at = k + (k >= low).astype(jnp.int32)
        others.append(at + (at >= high).astype(jnp.int32))
    return first, second, others


def at_block(block):
    return pl.ds(pl.multiple_of(block * BLOCK, BLOCK), BLOCK)


def pack_kernel(changed, wanted, items, accum, *refs):
    done, sent, chunks = refs[:4], refs[4], refs[5:]
    first, second, others = slots((wanted[0], wanted[1]))
    count = len(others) // 2

    def copy(block, kind, ref, at):
        rows = slice(at * BLOCK, (at + 1) * BLOCK)
        ref[rows, :] = (items, accum)[kind][at_block(block), :]
        for sub in range(INNER):

            @pl.when(block == changed[sub])
            def _():
                ref[rows, :] = done[2 * sub + kind][...]

    for kind in range(2):
        copy(first, kind, sent, kind)
        copy(second, kind, sent, 2 + kind)
        for k, block in enumerate(others):
            copy(block, kind, chunks[2 * kind + k // count], k % count)
    for k, block in enumerate((first, second)):
        at = count * BLOCK + 8 * k
        chunks[0][at : at + 8, :] = jnp.full((8, items.shape[1]), block.astype(jnp.float32))


def pack(changed, wanted, items, accum, done):
    width = items.shape[1]
    heights = [4 * BLOCK, 3 * BLOCK + 16] + [3 * BLOCK] * 3
    shapes = [(h, width) for h in heights]
    smem = pl.BlockSpec(memory_space=pltpu.SMEM)
    return pl.pallas_call(
        pack_kernel,
        grid=(1,),
        out_shape=[jax.ShapeDtypeStruct(shape, jnp.float32) for shape in shapes],
        in_specs=[smem, smem] + [whole(items.shape)] * 2 + [whole((BLOCK, width))] * 4,
        out_specs=[whole(shape) for shape in shapes],
        compiler_params=pltpu.CompilerParams(vmem_limit_bytes=VMEM_BYTES),
        cost_estimate=pl.CostEstimate(flops=0, bytes_accessed=4 * 2**20, transcendentals=0),
    )(changed, wanted, items, accum, *done)


def place_kernel(pair, got, *refs):
    chunks, tables = refs[:4], refs[4:]
    first, second, others = slots((pair[0], pair[1]))
    count = len(others) // 2
    for kind in range(2):
        for k, block in enumerate(others):
            rows = slice(k % count * BLOCK, (k % count + 1) * BLOCK)
            tables[kind][at_block(block), :] = chunks[2 * kind + k // count][rows, :]
        for k, block in enumerate((first, second)):
            at = (2 * k + kind) * BLOCK
            tables[kind][at_block(block), :] = got[at : at + BLOCK, :]


def place_all(pair, got, chunks):
    shape = (BLOCKS * BLOCK, got.shape[1])
    return pl.pallas_call(
        place_kernel,
        grid=(1,),
        out_shape=[jax.ShapeDtypeStruct(shape, jnp.float32)] * 2,
        in_specs=[pl.BlockSpec(memory_space=pltpu.SMEM), whole(got.shape)]
        + [whole(chunk.shape) for chunk in chunks],
        out_specs=[whole(shape)] * 2,
        compiler_params=pltpu.CompilerParams(vmem_limit_bytes=VMEM_BYTES),
        cost_estimate=pl.CostEstimate(flops=0, bytes_accessed=4 * 2**20, transcendentals=0),
    )(pair, got, *chunks)


def plan_kernel(partners, out):
    position = lax.axis_index("dom")
    level = []
    for bucket in range(BUCKETS):
        mask = partners[bucket, position] ^ position
        level.append(sum((mask >> bit & 1) * bit for bit in range(1, LEVELS)))
    low, high = jnp.minimum(*level), jnp.maximum(*level)
    out[0], out[1] = level
    out[2] = jnp.where(low == high, 0, 1 + high * (high - 1) // 2 + low)


def plan(partners):
    smem = pl.BlockSpec(memory_space=pltpu.SMEM)
    return pl.pallas_call(
        plan_kernel,
        out_shape=jax.ShapeDtypeStruct((3,), jnp.int32),
        in_specs=[smem],
        out_specs=smem,
    )(partners)


def shifted(value, step, flip):
    route = []
    for place in range(RING):
        for side in range(2):
            route.append((2 * place + side, 2 * ((place + step) % RING) + (side ^ flip)))
    return lax.ppermute(value, "grp", route)


def traded(value, mask):
    if not mask:
        return value
    count = lax.axis_size("dom")
    return lax.ppermute(value, "dom", [(d, d ^ mask) for d in range(count)])


def by_index(index, masks, act, *values):
    return lax.switch(index, [functools.partial(act, mask=m) for m in masks], *values)


def adagrad(param, accum, grad):
    accum = accum + grad * grad
    return (param - learn_rate * grad / (jnp.sqrt(accum) + epsilon), accum)


def crossed(value):
    return shifted(value, 0, 1)


def gathered(block, cross):
    near = [shifted(block, -step, 0) for step in STEPS]
    other = cross(block)
    far = [shifted(other, -step, 0) for step in STEPS]
    return [block] + near + [other] + far


def reduced(sums, cross):
    far = [shifted(sums[5 + k], step, 0) for k, step in enumerate(STEPS)]
    near = [shifted(sums[1 + k], step, 0) for k, step in enumerate(STEPS)]
    other = cross(sums[4] + far[0] + far[1] + far[2])
    return (sums[0] + near[0] + near[1] + near[2]) + other


def take(table, pick):
    return lax.dynamic_slice_in_dim(table, pick * BLOCK, BLOCK, 0)


def cross_beside(value, moving, index, masks):
    value, moving = lax.optimization_barrier((value, moving))
    other = crossed(value)
    moved = by_index(index, masks, traded, moving)
    return lax.optimization_barrier((other, moved))


def newest(again, new, old):
    return tuple(jnp.where(again, n, o) for n, o in zip(new, old))


def train(chosen, tables, half, targets, cross, into=(), full=False):
    blocks = gathered(chosen[0], cross)
    sums, users = train_call(targets, tables, half, blocks, into, full)
    return users, adagrad(chosen[0], chosen[1], reduced(sums, cross))


def body(user_table, user_accum, item_table, item_accum, block_pick, positives, partners):
    singles = [1 << i for i in range(LEVELS)]
    pairs = [0] + [1 << i | 1 << j for i in range(LEVELS) for j in range(i)]
    span = user_table.shape[0] // INNER
    targets = [
        [positives[bucket, sub].reshape(1, span) for sub in range(INNER)]
        for bucket in range(BUCKETS)
    ]
    picks = block_pick[:, :, 0]
    again = picks[:, 0] == picks[:, 1]
    tables = (item_table, item_accum)

    level = plan(partners)
    chosen = tuple(take(t, picks[0, 0]) for t in tables)
    users0, new0 = train(chosen, (user_table, user_accum), 0, targets[0][0], crossed)
    chosen = newest(again[0], new0, tuple(take(t, picks[0, 1]) for t in tables))
    wanted = []

    def cross_and_ask(value):
        if wanted:
            return crossed(value)
        other, asked = cross_beside(value, picks[1], level[0], singles)
        wanted.append(asked)
        return other

    users1, new1 = train(chosen, (user_table, user_accum), 1, targets[0][1], cross_and_ask)

    sent, *chunks = pack(picks[0], wanted[0], *tables, new0 + new1)
    got = by_index(level[0], singles, traded, sent)
    got = tuple(got[i * BLOCK : (i + 1) * BLOCK] for i in range(4))
    arrived = []

    def cross_and_send(value):
        other, chunk = cross_beside(value, chunks[len(arrived)], level[2], pairs)
        arrived.append(chunk)
        return other

    users, new0 = train(got[:2], users0, 0, targets[1][0], cross_and_send, full=True)
    chosen = newest(again[1], new0, got[2:])
    users, new1 = train(
        chosen, users1, 1, targets[1][1], cross_and_send, into=users, full=True
    )

    last = newest(again[1], new1, new0) + newest(again[1], got[2:], new1)
    got = by_index(level[1], singles, traded, jnp.concatenate(last))
    at = arrived[0].shape[0] - 16
    pair = arrived[0][at::8, 0].astype(jnp.int32)
    return users + tuple(place_all(pair, got, arrived))


def solution(mesh):
    placed = (
        P(("grp", "dom"), None),
        P(("grp", "dom"), None),
        P(("grp", "dom"), None),
        P(("grp", "dom"), None),
        P(None, None, ("grp", "dom")),
        P(None, None, ("grp", "dom")),
        P(),
    )
    return jax.shard_map(
        body,
        mesh=mesh,
        in_specs=placed,
        out_specs=(P(("grp", "dom"), None),) * 4,
        check_vma=False,
    )
```
